32 devices in a mesh: row: 16 (over z, y, x), col: 2 (over core).
Axes of the slice: x: 2, y: 2, z: 4, core: 2. Of those that a mesh axis runs over, the one named last changes fastest.
Arguments:
- near_blocks: float32 [128, 2, 256, 256], P('row', 'col'), may hold values from -0.25 to 0.25
- column_block: int32 [128, 2], P('row', 'col'), may hold values from 0 to 127, as said below
- test_panels: float32 [128, 256, 256], P(('row', 'col')), may hold values from -6 to 6
- nugget: float32 [128, 256], P('row'), may hold values from 0.5 to 2
Outputs:
- leaf_basis: float32 [128, 128, 256], P('row', None, 'col')
- leaf_miss: float32 [128, 128, 256], P('row', None, 'col')
- local_basis: float32 [112, 128, 256], P('row', None, 'col')
- upper_basis: float32 [16, 128, 256], P('row', None, 'col')
The draws below stay inside these ranges and needn't reach their ends.
Inputs may be any that keep to these rules, and one draw needn't show every extreme that they name: `column_block`: row i names 2 different leaf blocks, i itself among them, all within i - 8 to i + 8.
All inputs are finite; a program needn't handle non-finite values.
Results may differ from the reference program's by a relative error of at most 0.0003.
Values sent between devices are 32-bit elements; how exact they have to be, the bound alone decides.
A program may use at most 64 MiB of HBM per device.

```python
import math
import jax
import jax.numpy as jnp
import numpy as np
from jax import lax

BLOCK = 256
PANEL = 128
LEAF_DEV = 8
NEAR = 2
LEAVES = 128
LEVELS_UP = 4
N_ROW = 16


def draw_column_block(key, part):
    window = 2 * LEAF_DEV + 1
    leaf_index = jnp.arange(LEAVES, dtype=jnp.int32)[:, None]
    offsets = jnp.arange(window, dtype=jnp.int32)[None, :] - LEAF_DEV
    target = leaf_index + offsets
    valid = (target >= 0) & (target < LEAVES)
    first_key = jax.random.fold_in(key, 11)
    second_key = jax.random.fold_in(key, 23)
    noise = jax.random.randint(first_key, (LEAVES, window), 0, 1 << 20)
    scores = noise * window + jnp.arange(window, dtype=jnp.int32)[None, :]
    scores = jnp.where(valid, scores, -1)
    scores = jnp.where(offsets == 0, (1 << 20) * window + window, scores)
    chosen_scores, chosen = lax.top_k(scores, NEAR)
    picked = jnp.take_along_axis(target, chosen, axis=1)
    shuffle = jax.random.randint(second_key, (LEAVES, NEAR), 0, 1 << 20) * NEAR + jnp.arange(NEAR, dtype=jnp.int32)[None, :]
    order_scores, order = lax.top_k(shuffle, NEAR)
    return jnp.take_along_axis(picked, order, axis=1).astype(jnp.int32)


def draw_test_panels(key, part):
    base_key = jax.random.fold_in(key, 31)
    sign_key = jax.random.fold_in(key, 37)
    column_key = jax.random.fold_in(key, 41)
    shape = (LEAVES, BLOCK, 2 * PANEL)
    base = jax.random.normal(base_key, shape, jnp.float32)
    signs = jax.random.randint(sign_key, (LEAVES, BLOCK, 1), 0, 2).astype(jnp.float32) * 2.0 - 1.0
    shared = jax.random.normal(column_key, (1, 1, 2 * PANEL), jnp.float32)
    return jnp.clip(base + signs * shared, -6.0, 6.0).astype(jnp.float32)


def shard_levels(stream_key, shape, shards, least, top_value):
    def one(axis_at, blocks):
        draws = jax.random.uniform(jax.random.fold_in(jax.random.fold_in(stream_key, 6), axis_at), (blocks,), jnp.float32, least / len(shards), top_value / len(shards))
        return jnp.repeat(jnp.exp(draws), shape[axis_at] // blocks).reshape((-1,) + (1,) * (len(shape) - axis_at - 1))

    level = one(*shards[0])
    for cut in shards[1:]:
        level = level * one(*cut)
    return level


def bell_draw(key, extent, deviation, bound, split=(), held_as=jnp.bfloat16):
    entries = jax.random.normal(key, extent, jnp.float32) * deviation
    if len(split) > 0:
        entries = shard_levels(key, extent, split, -0.22, 0.18) * entries
    return jnp.clip(entries, min=-bound, max=bound).astype(held_as)


def setup_inputs(seed: int = 0) -> dict:
    seeds = jax.random.split(jax.random.key(seed), 5)
    return {
        "near_blocks": bell_draw(seeds[0], (LEAVES, NEAR, BLOCK, BLOCK), (BLOCK * NEAR) ** -0.5, 0.25, ((0, 16), (1, 2)), jnp.float32),
        "column_block": draw_column_block(jax.random.fold_in(seeds[4], 71), 0),
        "test_panels": draw_test_panels(jax.random.fold_in(seeds[4], 71), 0),
        "nugget": jnp.clip(jnp.exp(math.log(2.0) - 1.3862944 * jax.random.uniform(seeds[3], (LEAVES, BLOCK), jnp.float32) ** shard_levels(seeds[3], (LEAVES, BLOCK), ((0, 16),), -0.2, 0.2)), 0.5, 2.0),
    }


def product(left, right):
    return jnp.matmul(left, right, precision=lax.Precision.HIGHEST)

def combine(factor_a, panel_a, factor_b, panel_b):
    gram_matrix = product(factor_a, jnp.swapaxes(factor_a, -1, -2)) + product(factor_b, jnp.swapaxes(factor_b, -1, -2))
    factor = jnp.linalg.cholesky(gram_matrix)
    basis_node = jax.scipy.linalg.solve_triangular(factor, jnp.concatenate([factor_a, factor_b], axis=-1), lower=True)
    reduced = jax.scipy.linalg.solve_triangular(factor, product(factor_a, panel_a) + product(factor_b, panel_b), lower=True)
    return (basis_node, factor, reduced)

def reference(near_blocks, column_block, test_panels, nugget):

    def one_leaf(leaf_index):
        blocks = near_blocks[leaf_index]
        picked = jnp.take(test_panels, column_block[leaf_index], axis=0)
        total = jnp.einsum('kab,kbs->as', blocks, picked, precision=lax.Precision.HIGHEST)
        return total + nugget[leaf_index][:, None] * test_panels[leaf_index]
    sample = lax.map(one_leaf, jnp.arange(LEAVES, dtype=jnp.int32))
    panel_one = sample[:, :, :PANEL]
    panel_two = sample[:, :, PANEL:]
    gram_matrix = jnp.einsum('las,lat->lst', panel_one, panel_one, precision=lax.Precision.HIGHEST)
    cross_gram = jnp.einsum('las,lat->lst', panel_one, panel_two, precision=lax.Precision.HIGHEST)
    factor = jnp.linalg.cholesky(gram_matrix)
    leaf_basis = jax.scipy.linalg.solve_triangular(factor, jnp.swapaxes(panel_one, 1, 2), lower=True)
    reduced = jax.scipy.linalg.solve_triangular(factor, cross_gram, lower=True)
    leaf_miss = jnp.swapaxes(panel_two, 1, 2) - jnp.einsum('lst,lsa->lta', reduced, leaf_basis, precision=lax.Precision.HIGHEST)
    levels_local = LEAF_DEV.bit_length() - 1
    local_parts = []
    upper_basis = jnp.zeros((N_ROW, PANEL, 2 * PANEL), jnp.float32)
    current_factor, current_panel = (factor, reduced)
    for level_index in range(levels_local + LEVELS_UP):
        pair_count = current_factor.shape[0] // 2
        pair_factor = current_factor.reshape(pair_count, 2, PANEL, PANEL)
        pair_panel = current_panel.reshape(pair_count, 2, PANEL, PANEL)
        basis_level, current_factor, current_panel = combine(pair_factor[:, 0], pair_panel[:, 0], pair_factor[:, 1], pair_panel[:, 1])
        if level_index < levels_local:
            local_parts.append(basis_level.reshape(N_ROW, -1, PANEL, 2 * PANEL))
        else:
            rise = level_index - levels_local + 1
            target_rows = np.arange(pair_count, dtype=np.int32) * 2 ** rise + 2 ** (rise - 1)
            upper_basis = upper_basis.at[target_rows].set(basis_level)
    root_scale = 1.0 / math.sqrt(LEAVES * BLOCK)
    root_stack = jnp.concatenate([jnp.swapaxes(current_factor[0], 0, 1), current_panel[0]], axis=1) * root_scale
    upper_basis = upper_basis.at[0].set(root_stack)
    local_basis = jnp.concatenate(local_parts, axis=1).reshape(N_ROW * (LEAF_DEV - 1), PANEL, 2 * PANEL)
    return (leaf_basis, leaf_miss, local_basis, upper_basis)
```

```python
import functools
import math

import jax
import jax.numpy as jnp
from jax import lax
from jax.experimental import pallas as pl
from jax.experimental.pallas import tpu as pltpu
from jax.sharding import PartitionSpec as P

STRIP = 32
SLAB = 8
LIMIT = 48 * 1024 * 1024


def dot(left, right, left_dim, right_dim):
    return lax.dot_general(
        left,
        right,
        (((left_dim,), (right_dim,)), ((), ())),
        precision=lax.Precision.HIGHEST,
        preferred_element_type=jnp.float32,
    )


def load_augmented(work, slot, gram):
    size = gram.shape[0]
    row = lax.broadcasted_iota(jnp.int32, (size, size), 0)
    lane = lax.broadcasted_iota(jnp.int32, (size, size), 1)
    work[slot, :, :size] = gram
    work[slot, :, size:] = jnp.where(row == lane, 1.0, 0.0)


def eliminate(work, first, count):
    size = work.shape[1]
    row = lax.broadcasted_iota(jnp.int32, (count, SLAB, 1), 1)
    lane = lax.broadcasted_iota(jnp.int32, (1, SLAB, 2 * size), 2)
    sub = lax.broadcasted_iota(jnp.int32, (1, SLAB, 2 * size), 1)
    own = pl.ds(first, count)
    for top in range(0, size, STRIP):
        slabs = [
            work[own, top + at : top + at + SLAB, :] for at in range(0, STRIP, SLAB)
        ]
        for step in range(STRIP):
            at, inner = divmod(step, SLAB)
            here = top + step
            column = slabs[at][:, :, here : here + 1]
            pivot_row = slabs[at][:, inner : inner + 1, :]
            pivot = column[:, inner : inner + 1, :]
            scaled = pivot_row * (1.0 / pivot)
            for later in range(at, len(slabs)):
                if later == at:
                    if inner == SLAB - 1:
                        continue
                    factor = jnp.where(row > inner, column, 0.0)
                else:
                    factor = slabs[later][:, :, here : here + 1]
                slabs[later] = slabs[later] - factor * scaled
        done = []
        for at, slab in enumerate(slabs):
            base = top + at * SLAB
            diagonal = jnp.sum(
                jnp.where(lane == sub + base, slab, 0.0), axis=2, keepdims=True
            )
            slab = slab * lax.rsqrt(diagonal)
            slab = jnp.where(lane >= sub + base, slab, 0.0)
            work[own, base : base + SLAB, :] = slab
        below = top + STRIP
        if below < size:
            for slot in range(first, first + count):
                strip = work[slot, top:below, :]
                work[slot, below:, :] -= dot(strip[:, below:size], strip, 0, 0)


def sample_kernel(place, near, panels, own, nugget, sample, moments, total):
    leaf, slot = pl.program_id(0), pl.program_id(1)
    width = moments.shape[1]
    part = dot(near[0, 0], panels[0], 1, 0)

    @pl.when(slot == 0)
    def _():
        sample[0] = part + own[0] * nugget[0]

    @pl.when(slot > 0)
    def _():
        sample[0] += part

    @pl.when(slot == pl.num_programs(1) - 1)
    def _():
        whole = sample[0]
        both = dot(whole[:, :width], whole, 0, 0)
        moments[0] = both

        @pl.when(leaf == 0)
        def _():
            total[...] = both

        @pl.when(leaf > 0)
        def _():
            total[...] += both


def sampled(near, place, panels, own_place, nugget):
    slots, leaves, block, _ = near.shape
    wide = panels.shape[2]
    width = wide // 2
    grid = pltpu.PrefetchScalarGridSpec(
        num_scalar_prefetch=1,
        grid=(leaves, slots),
        in_specs=[
            pl.BlockSpec((1, 1, block, block), lambda i, k, p: (k, i, 0, 0)),
            pl.BlockSpec((1, block, wide), lambda i, k, p: (p[i * (slots + 1) + k], 0, 0)),
            pl.BlockSpec((1, block, wide), lambda i, k, p: (p[i * (slots + 1) + slots], 0, 0)),
            pl.BlockSpec((1, block, 1), lambda i, k, p: (i, 0, 0)),
        ],
        out_specs=[
            pl.BlockSpec((1, block, wide), lambda i, k, p: (i, 0, 0)),
            pl.BlockSpec((1, width, wide), lambda i, k, p: (i, 0, 0)),
            pl.BlockSpec((width, wide), lambda i, k, p: (0, 0)),
        ],
    )
    index = jnp.concatenate([place.T, own_place[:, None]], axis=1).reshape(-1)
    return pl.pallas_call(
        sample_kernel,
        grid_spec=grid,
        out_shape=[
            jax.ShapeDtypeStruct((leaves, block, wide), jnp.float32),
            jax.ShapeDtypeStruct((leaves, width, wide), jnp.float32),
            jax.ShapeDtypeStruct((width, wide), jnp.float32),
        ],
        compiler_params=pltpu.CompilerParams(vmem_limit_bytes=LIMIT),
    )(index, near, panels, panels, nugget[:, :, None])


def local_kernel(columns, sample, moments, basis, missed, inner, work, sums):
    leaves, width, wide = moments.shape
    share = wide // columns
    column = lax.axis_index("col")
    side = column * share // width
    offset = pl.multiple_of(column * share % width, share)
    nodes = 2 * leaves - 1
    for leaf in range(leaves):
        sums[leaf] = moments[leaf, :, :width]
    for node in range(leaves, nodes):
        child = 2 * (node - leaves)
        sums[node] = sums[child] + sums[child + 1]
    for node in range(nodes):
        load_augmented(work, node, sums[node])
    eliminate(work, 0, nodes)
    points = pl.ds(pl.multiple_of(column * share, share), share)
    for leaf in range(leaves):
        inverse = work[leaf, :, width:]
        part = sample[leaf, points, :]
        own = dot(inverse, part[:, :width], 1, 1)
        basis[leaf] = own
        reduced = dot(inverse, moments[leaf, :, width:], 1, 0)
        missed[leaf] = part[:, width:].T - dot(reduced, own, 0, 0)
    for node in range(leaves, nodes):
        child = 2 * (node - leaves) + side
        inner[node - leaves] = dot(
            work[node, :, width:], work[child, pl.ds(offset, share), :width], 1, 1
        )


def upper_kernel(columns, scale, pair, root, upper, work):
    width, wide = root.shape[0], 2 * root.shape[0]
    share = wide // columns
    column = lax.axis_index("col")
    offset = pl.multiple_of(column * share % width, share)
    load_augmented(work, 0, pair[0])
    load_augmented(work, 1, pair[1])
    eliminate(work, 0, 2)
    inverse = work[0, :, width:]
    node = dot(inverse, work[1, pl.ds(offset, share), :width], 1, 1)
    top = dot(inverse, root[...], 1, 0) * scale
    upper[0] = jnp.where(lax.axis_index("row") == 0, top, node)


def whole_spec():
    return pl.BlockSpec(memory_space=pltpu.VMEM)


def local_bases(sample, moments, columns):
    leaves, width, wide = moments.shape
    share = wide // columns
    nodes = 2 * leaves - 1
    return pl.pallas_call(
        functools.partial(local_kernel, columns),
        in_specs=[whole_spec()] * 2,
        out_specs=[whole_spec()] * 3,
        out_shape=[
            jax.ShapeDtypeStruct((leaves, width, share), jnp.float32),
            jax.ShapeDtypeStruct((leaves, width, share), jnp.float32),
            jax.ShapeDtypeStruct((leaves - 1, width, share), jnp.float32),
        ],
        scratch_shapes=[
            pltpu.VMEM((nodes, width, wide), jnp.float32),
            pltpu.VMEM((nodes, width, width), jnp.float32),
        ],
        compiler_params=pltpu.CompilerParams(vmem_limit_bytes=LIMIT),
        cost_estimate=pl.CostEstimate(
            flops=10_000_000_000, bytes_accessed=4_000_000, transcendentals=0
        ),
    )(sample, moments)


def upper_bases(pair, root, columns, scale):
    width, wide = root.shape[0], 2 * root.shape[0]
    share = wide // columns
    return pl.pallas_call(
        functools.partial(upper_kernel, columns, scale),
        in_specs=[whole_spec()] * 2,
        out_specs=whole_spec(),
        out_shape=jax.ShapeDtypeStruct((1, width, share), jnp.float32),
        scratch_shapes=[pltpu.VMEM((2, width, wide), jnp.float32)],
        compiler_params=pltpu.CompilerParams(vmem_limit_bytes=LIMIT),
    )(pair, root)


def around(block, axis):
    count = lax.axis_size(axis)
    parts = [block]
    for shift in range(1, count):
        route = [((i + shift) % count, i) for i in range(count)]
        parts.append(lax.ppermute(block, axis, route))
    return parts


def on_device(near_blocks, column_block, test_panels, nugget):
    leaves = near_blocks.shape[0]
    block = near_blocks.shape[2]
    width = test_panels.shape[2] // 2
    piece = test_panels.shape[0]
    row = lax.axis_index("row")
    column = lax.axis_index("col")
    rows = lax.axis_size("row")
    columns = lax.axis_size("col")

    near = jnp.stack(around(near_blocks[:, 0], "col"))
    choice = jnp.stack(around(column_block[:, 0], "col"))
    forward = [(i, i + 1) for i in range(rows - 1)]
    backward = [(i + 1, i) for i in range(rows - 1)]
    low = lax.ppermute(test_panels, "row", forward)
    high = lax.ppermute(test_panels, "row", backward)
    panels = jnp.concatenate([low, test_panels, high], axis=0)
    panels = jnp.concatenate(around(panels, "col"), axis=0)

    def position(index):
        part, within = index // leaves, index % leaves
        shift = (within // piece - column + columns) % columns
        return shift * (3 * piece) + part * piece + within % piece

    place = position(choice - (row - 1) * leaves)
    own_place = position(jnp.arange(leaves, dtype=jnp.int32) + leaves)
    sample, moments, total = sampled(near, place, panels, own_place, nugget)

    basis, missed, inner = local_bases(sample, moments, columns)

    share = 2 * width // columns
    on_left = column * share // width == 0
    node, child = total[:, :width], total[:, :width]
    for level in range(rows.bit_length() - 1):
        stride = 1 << level
        route = [(i, i ^ stride) for i in range(rows)]
        other = lax.ppermute(total, "row", route)
        both = total + other
        here = row % (2 * stride) == stride
        node = jnp.where(here, both[:, :width], node)
        child = jnp.where(here, jnp.where(on_left, other, total)[:, :width], child)
        total = both
    node = jnp.where(row == 0, total[:, :width], node)
    root = lax.dynamic_slice_in_dim(total, column * share, share, 1)
    scale = 1.0 / math.sqrt(leaves * rows * block)
    upper = upper_bases(jnp.stack([node, child]), root, columns, scale)
    return (basis, missed, inner, upper)


def solution(mesh):
    placed = (
        P("row", "col", None, None),
        P("row", "col"),
        P(("row", "col"), None, None),
        P("row", None),
    )
    return jax.shard_map(
        on_device,
        mesh=mesh,
        in_specs=placed,
        out_specs=(P("row", None, "col"),) * 4,
        check_vma=False,
    )
```

```python
import functools
import math

import jax
import jax.numpy as jnp
from jax import lax
from jax.experimental import pallas as pl
from jax.experimental.pallas import tpu as pltpu
from jax.sharding import PartitionSpec as P

STRIP = 32
SLAB = 8
CUTS = 2
LIMIT = 48 * 1024 * 1024


def dot(left, right, left_dim, right_dim):
    return lax.dot_general(
        left,
        right,
        (((left_dim,), (right_dim,)), ((), ())),
        precision=lax.Precision.HIGHEST,
        preferred_element_type=jnp.float32,
    )


def load_augmented(work, slot, gram):
    size = gram.shape[0]
    row = lax.broadcasted_iota(jnp.int32, (size, size), 0)
    lane = lax.broadcasted_iota(jnp.int32, (size, size), 1)
    work[slot, :, :size] = gram
    work[slot, :, size:] = jnp.where(row == lane, 1.0, 0.0)


def eliminate(work, first, count):
    size = work.shape[1]
    row = lax.broadcasted_iota(jnp.int32, (count, SLAB, 1), 1)
    lane = lax.broadcasted_iota(jnp.int32, (1, SLAB, 2 * size), 2)
    sub = lax.broadcasted_iota(jnp.int32, (1, SLAB, 2 * size), 1)
    own = pl.ds(first, count)
    for top in range(0, size, STRIP):
        slabs = [
            work[own, top + at : top + at + SLAB, :] for at in range(0, STRIP, SLAB)
        ]
        for step in range(STRIP):
            at, inner = divmod(step, SLAB)
            here = top + step
            column = slabs[at][:, :, here : here + 1]
            pivot_row = slabs[at][:, inner : inner + 1, :]
            pivot = column[:, inner : inner + 1, :]
            scaled = pivot_row * (1.0 / pivot)
            for later in range(at, len(slabs)):
                if later == at:
                    if inner == SLAB - 1:
                        continue
                    factor = jnp.where(row > inner, column, 0.0)
                else:
                    factor = slabs[later][:, :, here : here + 1]
                slabs[later] = slabs[later] - factor * scaled
        done = []
        for at, slab in enumerate(slabs):
            base = top + at * SLAB
            diagonal = jnp.sum(
                jnp.where(lane == sub + base, slab, 0.0), axis=2, keepdims=True
            )
            slab = slab * lax.rsqrt(diagonal)
            slab = jnp.where(lane >= sub + base, slab, 0.0)
            work[own, base : base + SLAB, :] = slab
        below = top + STRIP
        if below < size:
            for slot in range(first, first + count):
                strip = work[slot, top:below, :]
                work[slot, below:, :] -= dot(strip[:, below:size], strip, 0, 0)


def peer(**place):
    return dict(device_id=place, device_id_type=pl.DeviceIdType.MESH)


def gather_kernel(
    rows, columns, pick, flag, near, test, nugget,
    sample, moments, pair, root,
    panels, blocks, sums, inbox,
    send_x, recv_x, send_y, recv_y, send_z, recv_z,
    send_c, recv_c, send_own, recv_own, send_near, recv_near, send_up, recv_up, here_sem,
):
    row, column = lax.axis_index("row"), lax.axis_index("col")
    leaves, size = near.shape[1], near.shape[2]
    piece = test.shape[0]
    width = moments.shape[1]
    levels = rows.bit_length() - 1
    corner = row % 4
    ends = jnp.logical_or(corner == 0, corner == 3)
    above = jnp.logical_and(ends, row + 4 < rows)
    below = jnp.logical_and(ends, row >= 4)
    z_out = jnp.where(corner == 0, row + 4, row - 4)
    has_out = jnp.where(corner == 0, above, below)
    has_in = jnp.where(corner == 0, below, above)

    barrier = pltpu.get_barrier_semaphore()
    for level in range(levels):
        pl.semaphore_signal(barrier, inc=1, **peer(row=row ^ (1 << level)))
    for shift in range(1, columns):
        pl.semaphore_signal(barrier, inc=1, **peer(col=(column + shift) % columns))

    @pl.when(above)
    def _():
        pl.semaphore_signal(barrier, inc=1, **peer(row=row + 4))

    @pl.when(below)
    def _():
        pl.semaphore_signal(barrier, inc=1, **peer(row=row - 4))

    extra = above.astype(jnp.int32) + below.astype(jnp.int32)
    pl.semaphore_wait(barrier, levels + columns - 1 + extra)

    cuts = CUTS
    part_rows = size // cuts
    chunks = piece * cuts

    def part(ref, *lead_and_chunk):
        *lead, chunk = lead_and_chunk
        at, cut = divmod(chunk, cuts)
        return ref.at[(*lead, at, pl.ds(cut * part_rows, part_rows))]

    def along(source, kind, chunk, send, recv, target):
        return pltpu.make_async_remote_copy(
            src_ref=source, dst_ref=part(panels, 0, kind, chunk),
            send_sem=send.at[chunk], recv_sem=recv.at[chunk], **peer(row=target),
        )

    def x_copy(chunk):
        return along(part(test, chunk), 1, chunk, send_x, recv_x, row ^ 1)

    def y_copy(chunk):
        return along(part(panels, 0, 1, chunk), 2, chunk, send_y, recv_y, row ^ 2)

    def z_copy(chunk):
        return along(part(panels, 0, 2, chunk), 3, chunk, send_z, recv_z, z_out)

    def c_copy(shift, kind, lane, chunk):
        return pltpu.make_async_remote_copy(
            src_ref=part(panels, 0, kind, chunk),
            dst_ref=part(panels, shift, kind, chunk),
            send_sem=send_c.at[shift - 1, lane, chunk],
            recv_sem=recv_c.at[shift - 1, lane, chunk],
            **peer(col=(column + shift) % columns),
        )

    def own_copy(shift):
        return pltpu.make_async_remote_copy(
            src_ref=test, dst_ref=panels.at[shift, 0],
            send_sem=send_own.at[shift - 1], recv_sem=recv_own.at[shift - 1],
            **peer(col=(column + shift) % columns),
        )

    def near_copy(shift):
        return pltpu.make_async_remote_copy(
            src_ref=near.at[0], dst_ref=blocks.at[shift],
            send_sem=send_near.at[shift - 1], recv_sem=recv_near.at[shift - 1],
            **peer(col=(column + shift) % columns),
        )

    shifts = range(1, columns)
    for chunk in range(chunks):
        x_copy(chunk).start()
    for shift in shifts:
        own_copy(shift).start()
        near_copy(shift).start()
    own_test = pltpu.make_async_copy(test, panels.at[0, 0], here_sem.at[0])
    own_near = pltpu.make_async_copy(near.at[0], blocks.at[0], here_sem.at[1])
    own_test.start()
    own_near.start()
    for step in range(chunks + 2):
        if step < chunks:
            x_copy(step).wait_recv()
            y_copy(step).start()
            for shift in shifts:
                c_copy(shift, 1, 0, step).start()
        if 1 <= step <= chunks:
            chunk = step - 1
            y_copy(chunk).wait_recv()

            @pl.when(has_out)
            def _():
                z_copy(chunk).start()

            @pl.when(jnp.logical_not(ends))
            def _():
                for shift in shifts:
                    c_copy(shift, 2, 1, chunk).start()

        if step >= 2:
            chunk = step - 2

            @pl.when(has_in)
            def _():
                z_copy(chunk).wait_recv()
                for shift in shifts:
                    c_copy(shift, 3, 1, chunk).start()

    for chunk in range(chunks):
        x_copy(chunk).wait_send()
        y_copy(chunk).wait_send()
        for shift in shifts:
            c_copy(shift, 1, 0, chunk).wait()

        @pl.when(has_out)
        def _():
            z_copy(chunk).wait_send()

        @pl.when(jnp.logical_not(ends))
        def _():
            for shift in shifts:
                c_copy(shift, 2, 1, chunk).wait()

        @pl.when(has_in)
        def _():
            for shift in shifts:
                c_copy(shift, 3, 1, chunk).wait()

    for shift in shifts:
        own_copy(shift).wait()
        near_copy(shift).wait()
    own_test.wait()
    own_near.wait()

    diagonal = lax.broadcasted_iota(jnp.int32, (size, size), 0) == lax.broadcasted_iota(
        jnp.int32, (size, size), 1
    )
    sums[0] = jnp.zeros_like(sums[0])

    @pl.loop(0, leaves)
    def _(leaf):
        variance = jnp.where(diagonal, nugget[leaf], 0.0)
        whole = jnp.zeros((size, 2 * width), jnp.float32)
        for slot in range(columns):
            at = slot * leaves + leaf
            whole += dot(blocks[slot, leaf] + variance * flag[at], panels[
                pick[3 * at], pick[3 * at + 1], pick[3 * at + 2]], 1, 0)
        sample[leaf] = whole
        both = dot(whole[:, :width], whole, 0, 0)
        moments[leaf] = both
        sums[0] += both

    for level in range(levels):
        stride = 1 << level
        up = pltpu.make_async_remote_copy(
            src_ref=sums.at[level], dst_ref=inbox.at[level],
            send_sem=send_up.at[level], recv_sem=recv_up.at[level], **peer(row=row ^ stride),
        )
        up.start()
        up.wait()
        both = sums[level] + inbox[level]
        sums[level + 1] = both

        @pl.when(row % (2 * stride) == stride)
        def _():
            left = (column * 2) // columns == 0
            pair[0] = both[:, :width]
            pair[1] = jnp.where(left, inbox[level], sums[level])[:, :width]

    root[...] = sums[levels]

    @pl.when(row == 0)
    def _():
        pair[0] = sums[levels, :, :width]
        pair[1] = sums[levels, :, :width]


def gathered(pick, flag, near, test, nugget, rows, columns):
    leaves, size = near.shape[1], near.shape[2]
    piece, wide = test.shape[0], test.shape[2]
    width = wide // 2
    levels = rows.bit_length() - 1
    chunks = piece * CUTS
    f32 = jnp.float32
    dma = pltpu.SemaphoreType.DMA
    smem = pl.BlockSpec(memory_space=pltpu.SMEM)
    anywhere = pl.BlockSpec(memory_space=pl.ANY)
    return pl.pallas_call(
        functools.partial(gather_kernel, rows, columns),
        in_specs=[smem, smem, anywhere, anywhere, whole_spec()],
        out_specs=[whole_spec()] * 4,
        out_shape=[
            jax.ShapeDtypeStruct((leaves, size, wide), f32),
            jax.ShapeDtypeStruct((leaves, width, wide), f32),
            jax.ShapeDtypeStruct((2, width, width), f32),
            jax.ShapeDtypeStruct((width, wide), f32),
        ],
        scratch_shapes=[
            pltpu.VMEM((columns, 4, piece, size, wide), f32),
            pltpu.VMEM((columns, leaves, size, size), f32),
            pltpu.VMEM((levels + 1, width, wide), f32),
            pltpu.VMEM((levels, width, wide), f32),
        ]
        + [dma((chunks,))] * 6
        + [dma((columns - 1, 2, chunks))] * 2
        + [dma((columns - 1,))] * 4
        + [dma((levels,))] * 2
        + [dma((2,))],
        compiler_params=pltpu.CompilerParams(
            vmem_limit_bytes=LIMIT, collective_id=0, has_side_effects=True
        ),
    )(pick, flag, near, test, nugget)


def bases_kernel(
    columns, scale, sample, moments, pair, root, basis, missed, inner, upper, work, sums
):
    leaves, width, wide = moments.shape
    share = wide // columns
    column = lax.axis_index("col")
    side = column * share // width
    offset = pl.multiple_of(column * share % width, share)
    nodes = 2 * leaves - 1
    for leaf in range(leaves):
        sums[leaf] = moments[leaf, :, :width]
    for node in range(leaves, nodes):
        child = 2 * (node - leaves)
        sums[node] = sums[child] + sums[child + 1]
    for node in range(nodes):
        load_augmented(work, node, sums[node])
    load_augmented(work, nodes, pair[0])
    load_augmented(work, nodes + 1, pair[1])
    eliminate(work, 0, nodes + 2)
    points = pl.ds(pl.multiple_of(column * share, share), share)
    for leaf in range(leaves):
        inverse = work[leaf, :, width:]
        part = sample[leaf, points, :]
        own = dot(inverse, part[:, :width], 1, 1)
        basis[leaf] = own
        reduced = dot(inverse, moments[leaf, :, width:], 1, 0)
        missed[leaf] = part[:, width:].T - dot(reduced, own, 0, 0)
    for node in range(leaves, nodes):
        child = 2 * (node - leaves) + side
        inner[node - leaves] = dot(
            work[node, :, width:], work[child, pl.ds(offset, share), :width], 1, 1
        )
    inverse = work[nodes, :, width:]
    node = dot(inverse, work[nodes + 1, pl.ds(offset, share), :width], 1, 1)
    top = dot(inverse, root[...], 1, 0) * scale
    upper[0] = jnp.where(lax.axis_index("row") == 0, top, node)


def whole_spec():
    return pl.BlockSpec(memory_space=pltpu.VMEM)


def bases(sample, moments, pair, root, columns, scale):
    leaves, width, wide = moments.shape
    share = wide // columns
    nodes = 2 * leaves - 1
    counts = (leaves, leaves, leaves - 1, 1)
    return pl.pallas_call(
        functools.partial(bases_kernel, columns, scale),
        in_specs=[whole_spec()] * 4,
        out_specs=[whole_spec()] * 4,
        out_shape=[
            jax.ShapeDtypeStruct((count, width, share), jnp.float32) for count in counts
        ],
        scratch_shapes=[
            pltpu.VMEM((nodes + 2, width, wide), jnp.float32),
            pltpu.VMEM((nodes, width, width), jnp.float32),
        ],
        compiler_params=pltpu.CompilerParams(vmem_limit_bytes=LIMIT),
    )(sample, moments, pair, root)


def around(block, axis):
    count = lax.axis_size(axis)
    parts = [block]
    for shift in range(1, count):
        route = [((i + shift) % count, i) for i in range(count)]
        parts.append(lax.ppermute(block, axis, route))
    return parts


def on_device(near_blocks, column_block, test_panels, nugget):
    leaves = near_blocks.shape[0]
    block = near_blocks.shape[2]
    width = test_panels.shape[2] // 2
    piece = test_panels.shape[0]
    row = lax.axis_index("row")
    column = lax.axis_index("col")
    rows = lax.axis_size("row")
    columns = lax.axis_size("col")

    choice = jnp.stack(around(column_block[:, 0], "col"))
    first = row * leaves
    place = choice - first + leaves
    part, within = place // leaves, place % leaves
    corner = row % 4
    low = jnp.where(corner == 0, 3, jnp.where(corner == 2, 2, 1))
    high = jnp.where(corner == 3, 3, jnp.where(corner == 1, 2, 1))
    kind = jnp.where(part == 0, low, jnp.where(part == 1, 0, high))
    shift = (column - within // piece + columns) % columns
    pick = jnp.stack([shift, kind, within % piece], axis=-1).reshape(-1)
    own = first + jnp.arange(leaves, dtype=jnp.int32)
    flag = (choice == own).astype(jnp.float32).reshape(-1)
    sample, moments, pair, root = gathered(
        pick, flag, near_blocks.swapaxes(0, 1), test_panels, nugget[:, None], rows, columns
    )
    share = 2 * width // columns
    root = lax.dynamic_slice_in_dim(root, column * share, share, 1)
    scale = 1.0 / math.sqrt(leaves * rows * block)
    return tuple(bases(sample, moments, pair, root, columns, scale))


def solution(mesh):
    placed = (
        P("row", "col", None, None),
        P("row", "col"),
        P(("row", "col"), None, None),
        P("row", None),
    )
    return jax.shard_map(
        on_device,
        mesh=mesh,
        in_specs=placed,
        out_specs=(P("row", None, "col"),) * 4,
        check_vma=False,
    )
```

```python
import functools
import math

import jax
import jax.numpy as jnp
from jax import lax
from jax.experimental import pallas as pl
from jax.experimental.pallas import tpu as pltpu
from jax.sharding import PartitionSpec as P

STRIP = 32
SLAB = 8
CUTS = 2
GROUP = 2
LIMIT = 48 * 1024 * 1024


def dot(left, right, left_dim, right_dim):
    return lax.dot_general(
        left,
        right,
        (((left_dim,), (right_dim,)), ((), ())),
        precision=lax.Precision.HIGHEST,
        preferred_element_type=jnp.float32,
    )


def load_augmented(work, slot, gram):
    size = gram.shape[0]
    row = lax.broadcasted_iota(jnp.int32, (size, size), 0)
    lane = lax.broadcasted_iota(jnp.int32, (size, size), 1)
    work[slot, :, :size] = gram
    work[slot, :, size:] = jnp.where(row == lane, 1.0, 0.0)


def split(value):
    high = value.astype(jnp.bfloat16)
    return high, (value - high.astype(jnp.float32)).astype(jnp.bfloat16)


def dot_three(left, right, left_dim, right_dim):
    def one(a, b):
        return lax.dot_general(
            a, b, (((left_dim,), (right_dim,)), ((), ())), preferred_element_type=jnp.float32
        )

    left_high, left_low = split(left)
    right_high, right_low = split(right)
    return one(left_high, right_high) + (one(left_high, right_low) + one(left_low, right_high))


def eliminate_strip(work, first, count, top):
    size = work.shape[1]
    row = lax.broadcasted_iota(jnp.int32, (1, SLAB, size), 1)
    lane = lax.broadcasted_iota(jnp.int32, (1, SLAB, size), 2)
    own = pl.ds(first, count)
    shape = (count, SLAB, size)

    def spread(value):
        return jnp.broadcast_to(value, shape)

    slabs = [
        [
            work[own, top + at : top + at + SLAB, half : half + size]
            for half in (0, size)
        ]
        for at in range(0, STRIP, SLAB)
    ]
    for step in range(0, STRIP, GROUP):
        at, inner = divmod(step, SLAB)
        here = top + step
        columns = {
            later: [
                spread(slabs[later][0][:, :, here + k : here + k + 1]) for k in range(GROUP)
            ]
            for later in range(at, len(slabs))
        }
        pivots = [
            [
                spread(columns[at][k][:, inner + m : inner + m + 1, :]) if m >= k else None
                for m in range(GROUP)
            ]
            for k in range(GROUP)
        ]
        rows = [
            [spread(half[:, inner + k : inner + k + 1, :]) for half in slabs[at]]
            for k in range(GROUP)
        ]
        for k in range(GROUP):
            inverse = 1.0 / pivots[k][k]
            lower = {m: pivots[k][m] * inverse for m in range(k + 1, GROUP)}
            for t in range(k + 1, GROUP):
                for m in range(t, GROUP):
                    pivots[t][m] = pivots[t][m] - pivots[k][m] * lower[t]
                rows[t] = [x - lower[t] * y for x, y in zip(rows[t], rows[k])]
                for later in columns:
                    columns[later][t] = columns[later][t] - columns[later][k] * lower[t]
            scaled = [half * inverse for half in rows[k]]
            for later in columns:
                factor = columns[later][k]
                if later == at:
                    if inner + k == SLAB - 1:
                        continue
                    factor = jnp.where(row > inner + k, factor, 0.0)
                slabs[later] = [x - factor * y for x, y in zip(slabs[later], scaled)]
    for at, slab in enumerate(slabs):
        base = top + at * SLAB
        diagonal = jnp.sum(
            jnp.where(lane == row + base, slab[0], 0.0), axis=2, keepdims=True
        )
        scale = lax.rsqrt(diagonal)
        work[own, base : base + SLAB, :size] = jnp.where(lane >= row + base, slab[0] * scale, 0.0)
        work[own, base : base + SLAB, size:] = slab[1] * scale
    below = top + STRIP
    if below < size:
        for slot in range(first, first + count):
            strip = work[slot, top:below, :]
            work[slot, below:, :] -= dot(strip[:, below:size], strip, 0, 0)


def peer(**place):
    return dict(device_id=place, device_id_type=pl.DeviceIdType.MESH)


def sweep_kernel(
    rows, columns, scale, choice, near, test, nugget,
    basis, missed, inner_basis, upper,
    panels, blocks, sample, moments, sums, inbox, grams, work, pair,
    send_x, recv_x, send_y, recv_y, send_z, recv_z,
    send_c, recv_c, send_own, recv_own, send_near, recv_near, send_up, recv_up, here_sem,
):
    row, column = lax.axis_index("row"), lax.axis_index("col")
    leaves, size = near.shape[1], near.shape[2]
    piece = test.shape[0]
    width = moments.shape[1]
    levels = rows.bit_length() - 1
    corner = row % 4
    ends = jnp.logical_or(corner == 0, corner == 3)
    above = jnp.logical_and(ends, row + 4 < rows)
    below = jnp.logical_and(ends, row >= 4)
    z_out = jnp.where(corner == 0, row + 4, row - 4)
    has_out = jnp.where(corner == 0, above, below)
    has_in = jnp.where(corner == 0, below, above)

    barrier = pltpu.get_barrier_semaphore()
    for level in range(levels):
        pl.semaphore_signal(barrier, inc=1, **peer(row=row ^ (1 << level)))
    for shift in range(1, columns):
        pl.semaphore_signal(barrier, inc=1, **peer(col=(column + shift) % columns))

    @pl.when(above)
    def _():
        pl.semaphore_signal(barrier, inc=1, **peer(row=row + 4))

    @pl.when(below)
    def _():
        pl.semaphore_signal(barrier, inc=1, **peer(row=row - 4))

    extra = above.astype(jnp.int32) + below.astype(jnp.int32)
    pl.semaphore_wait(barrier, levels + columns - 1 + extra)

    cuts = CUTS
    part_rows = size // cuts
    chunks = piece * cuts

    def part(ref, *lead_and_chunk):
        *lead, chunk = lead_and_chunk
        at, cut = divmod(chunk, cuts)
        return ref.at[(*lead, at, pl.ds(cut * part_rows, part_rows))]

    def along(source, kind, chunk, send, recv, target):
        return pltpu.make_async_remote_copy(
            src_ref=source, dst_ref=part(panels, 0, kind, chunk),
            send_sem=send.at[chunk], recv_sem=recv.at[chunk], **peer(row=target),
        )

    def x_copy(chunk):
        return along(part(test, chunk), 1, chunk, send_x, recv_x, row ^ 1)

    def y_copy(chunk):
        return along(part(panels, 0, 1, chunk), 2, chunk, send_y, recv_y, row ^ 2)

    def z_copy(chunk):
        return along(part(panels, 0, 2, chunk), 3, chunk, send_z, recv_z, z_out)

    def c_copy(shift, kind, lane, chunk):
        return pltpu.make_async_remote_copy(
            src_ref=part(panels, 0, kind, chunk),
            dst_ref=part(panels, shift, kind, chunk),
            send_sem=send_c.at[shift - 1, lane, chunk],
            recv_sem=recv_c.at[shift - 1, lane, chunk],
            **peer(col=(column + shift) % columns),
        )

    def own_copy(shift):
        return pltpu.make_async_remote_copy(
            src_ref=test, dst_ref=panels.at[shift, 0],
            send_sem=send_own.at[shift - 1], recv_sem=recv_own.at[shift - 1],
            **peer(col=(column + shift) % columns),
        )

    def near_copy(shift):
        return pltpu.make_async_remote_copy(
            src_ref=near.at[0], dst_ref=blocks.at[shift],
            send_sem=send_near.at[shift - 1], recv_sem=recv_near.at[shift - 1],
            **peer(col=(column + shift) % columns),
        )

    shifts = range(1, columns)
    for chunk in range(chunks):
        x_copy(chunk).start()
    for shift in shifts:
        own_copy(shift).start()
        near_copy(shift).start()
    own_test = pltpu.make_async_copy(test, panels.at[0, 0], here_sem.at[0])
    own_near = pltpu.make_async_copy(near.at[0], blocks.at[0], here_sem.at[1])
    own_test.start()
    own_near.start()
    diagonal = lax.broadcasted_iota(jnp.int32, (size, size), 0) == lax.broadcasted_iota(
        jnp.int32, (size, size), 1
    )
    first = row * leaves

    def own_slot(leaf):
        slot = jnp.int32(0)
        for k in range(1, columns):
            slot = jnp.where(choice[k, leaf] == first + leaf, k, slot)
        return slot

    def own_product(leaf):
        variance = jnp.where(diagonal, nugget[pl.ds(leaf, 1), :], 0.0)
        holder = (column - leaf // piece + columns) % columns
        sample[leaf] = dot_three(
            blocks[own_slot(leaf), leaf] + variance, panels[holder, 0, leaf % piece], 1, 0
        )

    early = min(2, chunks + 1)
    share_leaves = -(-leaves // (chunks + 2 - early))
    for step in range(chunks + 2):
        if step == early:
            for shift in shifts:
                own_copy(shift).wait()
                near_copy(shift).wait()
            own_test.wait()
            own_near.wait()
        if step < chunks:
            x_copy(step).wait_recv()
            y_copy(step).start()
            for shift in shifts:
                c_copy(shift, 1, 0, step).start()
        if 1 <= step <= chunks:
            chunk = step - 1
            y_copy(chunk).wait_recv()

            @pl.when(has_out)
            def _():
                z_copy(chunk).start()

            @pl.when(jnp.logical_not(ends))
            def _():
                for shift in shifts:
                    c_copy(shift, 2, 1, chunk).start()

        if step >= 2:
            chunk = step - 2

            @pl.when(has_in)
            def _():
                z_copy(chunk).wait_recv()
                for shift in shifts:
                    c_copy(shift, 3, 1, chunk).start()

        if step >= early:
            start = (step - early) * share_leaves

            @pl.loop(start, min(start + share_leaves, leaves))
            def _(leaf):
                own_product(leaf)

    for chunk in range(chunks):
        x_copy(chunk).wait_send()
        y_copy(chunk).wait_send()
        for shift in shifts:
            c_copy(shift, 1, 0, chunk).wait()

        @pl.when(has_out)
        def _():
            z_copy(chunk).wait_send()

        @pl.when(jnp.logical_not(ends))
        def _():
            for shift in shifts:
                c_copy(shift, 2, 1, chunk).wait()

        @pl.when(has_in)
        def _():
            for shift in shifts:
                c_copy(shift, 3, 1, chunk).wait()

    corner_low = jnp.where(corner == 0, 3, jnp.where(corner == 2, 2, 1))
    corner_high = jnp.where(corner == 3, 3, jnp.where(corner == 1, 2, 1))
    grams_total = sums.at[0]
    grams_total[...] = jnp.zeros_like(grams_total)

    @pl.loop(0, leaves)
    def _(leaf):
        whole = sample[leaf]
        for other in range(1, columns):
            slot = lax.rem(own_slot(leaf) + other, columns)
            place = choice[slot, leaf] - first + leaves
            side, within = place // leaves, place % leaves
            kind = jnp.where(side == 0, corner_low, jnp.where(side == 1, 0, corner_high))
            holder = (column - within // piece + columns) % columns
            whole += dot_three(
                blocks[slot, leaf], panels[holder, kind, within % piece], 1, 0
            )
        sample[leaf] = whole
        both = dot(whole[:, :width], whole, 0, 0)
        moments[leaf] = both
        grams_total[...] += both

    share = 2 * width // columns
    side = column * share // width
    offset = pl.multiple_of(column * share % width, share)
    nodes = 2 * leaves - 1

    def climb(level):
        return pltpu.make_async_remote_copy(
            src_ref=sums.at[level], dst_ref=inbox.at[level],
            send_sem=send_up.at[level], recv_sem=recv_up.at[level],
            **peer(row=row ^ (1 << level)),
        )

    def arrive(level):
        stride = 1 << level
        climb(level).wait()
        both = sums[level] + inbox[level]
        sums[level + 1] = both
        if level + 1 < levels:
            climb(level + 1).start()

        @pl.when(row % (2 * stride) == stride)
        def _():
            load_augmented(pair, 0, both[:, :width])
            load_augmented(pair, 1, jnp.where(side == 0, inbox[level], sums[level])[:, :width])

    climb(0).start()
    for leaf in range(leaves):
        grams[leaf] = moments[leaf, :, :width]
    for node in range(leaves, nodes):
        child = 2 * (node - leaves)
        grams[node] = grams[child] + grams[child + 1]
    for node in range(nodes):
        load_augmented(work, node, grams[node])
    level = 0
    for top in range(0, width, STRIP):
        eliminate_strip(work, 0, nodes, top)
        if level < levels:
            arrive(level)
            level += 1
    while level < levels:
        arrive(level)
        level += 1

    @pl.when(row == 0)
    def _():
        load_augmented(pair, 0, sums[levels, :, :width])
        load_augmented(pair, 1, sums[levels, :, :width])

    points = pl.ds(pl.multiple_of(column * share, share), share)

    def leaf_out(leaf):
        inverse = work[leaf, :, width:]
        part_sample = sample[leaf, points, :]
        own = dot_three(inverse, part_sample[:, :width], 1, 1)
        basis[leaf] = own
        reduced = dot_three(inverse, moments[leaf, :, width:], 1, 0)
        missed[leaf] = part_sample[:, width:].T - dot_three(reduced, own, 0, 0)

    def node_out(node):
        child = 2 * (node - leaves) + side
        inner_basis[node - leaves] = dot_three(
            work[node, :, width:], work[child, pl.ds(offset, share), :width], 1, 1
        )

    jobs = [functools.partial(leaf_out, leaf) for leaf in range(leaves)]
    jobs += [functools.partial(node_out, node) for node in range(leaves, nodes)]
    strips = width // STRIP
    for at in range(strips):
        eliminate_strip(pair, 0, 2, at * STRIP)
        for job in jobs[at::strips]:
            job()
    inverse = pair[0, :, width:]
    total = sums[levels]
    if share % width:
        place_row = lax.broadcasted_iota(jnp.int32, (2 * width, share), 0)
        place_lane = lax.broadcasted_iota(jnp.int32, (2 * width, share), 1)
        chosen = jnp.where(place_row == place_lane + column * share, 1.0, 0.0)
        root = dot(total, chosen, 1, 0)
    else:
        root = jnp.where(side == 0, total[:, :width], total[:, width:])
    node = dot(inverse, pair[1, pl.ds(offset, share), :width], 1, 1)
    upper[0] = jnp.where(row == 0, dot(inverse, root, 1, 0) * scale, node)


def whole_spec():
    return pl.BlockSpec(memory_space=pltpu.VMEM)


def swept(choice, near, test, nugget, rows, columns, scale):
    leaves, size = near.shape[1], near.shape[2]
    piece, wide = test.shape[0], test.shape[2]
    width = wide // 2
    share = wide // columns
    nodes = 2 * leaves - 1
    levels = rows.bit_length() - 1
    chunks = piece * CUTS
    f32 = jnp.float32
    dma = pltpu.SemaphoreType.DMA
    smem = pl.BlockSpec(memory_space=pltpu.SMEM)
    anywhere = pl.BlockSpec(memory_space=pl.ANY)
    return pl.pallas_call(
        functools.partial(sweep_kernel, rows, columns, scale),
        in_specs=[smem, anywhere, anywhere, whole_spec()],
        out_specs=[whole_spec()] * 4,
        out_shape=[
            jax.ShapeDtypeStruct((count, width, share), f32)
            for count in (leaves, leaves, leaves - 1, 1)
        ],
        scratch_shapes=[
            pltpu.VMEM((columns, 4, piece, size, wide), f32),
            pltpu.VMEM((columns, leaves, size, size), f32),
            pltpu.VMEM((leaves, size, wide), f32),
            pltpu.VMEM((leaves, width, wide), f32),
            pltpu.VMEM((levels + 1, width, wide), f32),
            pltpu.VMEM((levels, width, wide), f32),
            pltpu.VMEM((nodes, width, width), f32),
            pltpu.VMEM((nodes, width, wide), f32),
            pltpu.VMEM((2, width, wide), f32),
        ]
        + [dma((chunks,))] * 6
        + [dma((columns - 1, 2, chunks))] * 2
        + [dma((columns - 1,))] * 4
        + [dma((levels,))] * 2
        + [dma((2,))],
        compiler_params=pltpu.CompilerParams(
            vmem_limit_bytes=LIMIT, collective_id=0, has_side_effects=True
        ),
    )(choice, near, test, nugget)


def around(block, axis):
    count = lax.axis_size(axis)
    parts = [block]
    for shift in range(1, count):
        route = [((i + shift) % count, i) for i in range(count)]
        parts.append(lax.ppermute(block, axis, route))
    return parts


def on_device(near_blocks, column_block, test_panels, nugget):
    leaves = near_blocks.shape[0]
    block = near_blocks.shape[2]
    rows = lax.axis_size("row")
    columns = lax.axis_size("col")
    choice = jnp.stack(around(column_block[:, 0], "col"))
    scale = 1.0 / math.sqrt(leaves * rows * block)
    outs = swept(
        choice, near_blocks.swapaxes(0, 1), test_panels, nugget, rows, columns, scale
    )
    return tuple(outs)


def solution(mesh):
    placed = (
        P("row", "col", None, None),
        P("row", "col"),
        P(("row", "col"), None, None),
        P("row", None),
    )
    return jax.shard_map(
        on_device,
        mesh=mesh,
        in_specs=placed,
        out_specs=(P("row", None, "col"),) * 4,
        check_vma=False,
    )
```

```python
import functools
import math

import jax
import jax.numpy as jnp
from jax import lax
from jax.experimental import pallas as pl
from jax.experimental.pallas import tpu as pltpu
from jax.sharding import PartitionSpec as P

STRIP = 32
SLAB = 8
CUTS = 2
GROUP = 4
LIMIT = 60 * 1024 * 1024


def dot(left, right, left_dim, right_dim):
    return lax.dot_general(
        left,
        right,
        (((left_dim,), (right_dim,)), ((), ())),
        precision=lax.Precision.HIGHEST,
        preferred_element_type=jnp.float32,
    )


def load_augmented(work, slot, gram):
    size = gram.shape[0]
    row = lax.broadcasted_iota(jnp.int32, (size, size), 0)
    lane = lax.broadcasted_iota(jnp.int32, (size, size), 1)
    work[slot, :, :size] = gram
    work[slot, :, size:] = jnp.where(row == lane, 1.0, 0.0)


def split(value):
    high = value.astype(jnp.bfloat16)
    return high, (value - high.astype(jnp.float32)).astype(jnp.bfloat16)


def dot_three(left, right, left_dim, right_dim):
    def one(a, b):
        return lax.dot_general(
            a, b, (((left_dim,), (right_dim,)), ((), ())), preferred_element_type=jnp.float32
        )

    left_high, left_low = split(left)
    right_high, right_low = split(right)
    return one(left_high, right_high) + (one(left_high, right_low) + one(left_low, right_high))


def eliminate_strip(work, first, count, top):
    size = work.shape[1]
    row = lax.broadcasted_iota(jnp.int32, (1, SLAB, size), 1)
    lane = lax.broadcasted_iota(jnp.int32, (1, SLAB, size), 2)
    own = pl.ds(first, count)
    shape = (count, SLAB, size)

    def spread(value):
        return jnp.broadcast_to(value, shape)

    slabs = [
        [
            work[own, top + at : top + at + SLAB, half : half + size]
            for half in (0, size)
        ]
        for at in range(0, STRIP, SLAB)
    ]
    for step in range(0, STRIP, GROUP):
        at, inner = divmod(step, SLAB)
        here = top + step
        columns = {
            later: [
                spread(slabs[later][0][:, :, here + k : here + k + 1]) for k in range(GROUP)
            ]
            for later in range(at, len(slabs))
        }
        pivots = [
            [
                spread(columns[at][k][:, inner + m : inner + m + 1, :]) if m >= k else None
                for m in range(GROUP)
            ]
            for k in range(GROUP)
        ]
        rows = [
            [spread(half[:, inner + k : inner + k + 1, :]) for half in slabs[at]]
            for k in range(GROUP)
        ]
        for k in range(GROUP):
            inverse = 1.0 / pivots[k][k]
            lower = {m: pivots[k][m] * inverse for m in range(k + 1, GROUP)}
            for t in range(k + 1, GROUP):
                for m in range(t, GROUP):
                    pivots[t][m] = pivots[t][m] - pivots[k][m] * lower[t]
                rows[t] = [x - lower[t] * y for x, y in zip(rows[t], rows[k])]
                for later in columns:
                    columns[later][t] = columns[later][t] - columns[later][k] * lower[t]
            scaled = [half * inverse for half in rows[k]]
            for later in columns:
                factor = columns[later][k]
                if later == at:
                    if inner + k == SLAB - 1:
                        continue
                    factor = jnp.where(row > inner + k, factor, 0.0)
                slabs[later] = [x - factor * y for x, y in zip(slabs[later], scaled)]
    for at, slab in enumerate(slabs):
        base = top + at * SLAB
        diagonal = jnp.sum(
            jnp.where(lane == row + base, slab[0], 0.0), axis=2, keepdims=True
        )
        scale = lax.rsqrt(diagonal)
        work[own, base : base + SLAB, :size] = jnp.where(lane >= row + base, slab[0] * scale, 0.0)
        work[own, base : base + SLAB, size:] = slab[1] * scale
    below = top + STRIP
    if below < size:
        for slot in range(first, first + count):
            strip = work[slot, top:below, :]
            work[slot, below:, :] -= dot(strip[:, below:size], strip, 0, 0)


def eliminate_packed(work, count, top):
    size = work.shape[1]
    below = top + STRIP
    row = lax.broadcasted_iota(jnp.int32, (1, SLAB, size), 1)
    lane = lax.broadcasted_iota(jnp.int32, (1, SLAB, size), 2)
    own = pl.ds(0, count)
    shape = (count, SLAB, size)
    slabs = [work[own, top + at : top + at + SLAB, :] for at in range(0, STRIP, SLAB)]
    pivots = [None] * len(slabs)
    for step in range(STRIP):
        at, inner = divmod(step, SLAB)
        here = top + step
        columns = [
            jnp.broadcast_to(slab[:, :, here : here + 1], shape) for slab in slabs[at:]
        ]
        pivot = jnp.broadcast_to(columns[0][:, inner : inner + 1, :], shape)
        inverse = 1.0 / pivot
        pivots[at] = pivot if inner == 0 else jnp.where(row >= inner, pivot, pivots[at])
        pivot_row = jnp.broadcast_to(slabs[at][:, inner : inner + 1, :], shape)
        scaled = jnp.where(lane == here, 1.0, pivot_row) * inverse
        for later in range(at, len(slabs)):
            factor, slab = columns[later - at], slabs[later]
            if later == at:
                factor = jnp.where(row > inner, factor, 0.0)
                keep = jnp.where(row > inner, 0.0, jnp.where(row == inner, 1.0, slab))
                slab = jnp.where(lane == here, keep, slab)
            else:
                slab = jnp.where(lane == here, 0.0, slab)
            slabs[later] = slab - factor * scaled
    for at, slab in enumerate(slabs):
        base = top + at * SLAB
        work[own, base : base + SLAB, :] = slab * lax.rsqrt(pivots[at])
    if below < size:
        strip_row = lax.broadcasted_iota(jnp.int32, (STRIP, size), 0) + top
        strip_lane = lax.broadcasted_iota(jnp.int32, (STRIP, size), 1)
        hide = jnp.logical_and(strip_lane < below, strip_lane > strip_row)
        rest_lane = lax.broadcasted_iota(jnp.int32, (size - below, size), 1)
        cleared = jnp.logical_and(rest_lane >= top, rest_lane < below)
        for slot in range(count):
            strip = work[slot, top:below, :]
            rest = jnp.where(cleared, 0.0, work[slot, below:, :])
            work[slot, below:, :] = rest - dot(
                strip[:, below:size], jnp.where(hide, 0.0, strip), 0, 0
            )


def inverse_of(packed):
    row = lax.broadcasted_iota(jnp.int32, packed.shape, 0)
    lane = lax.broadcasted_iota(jnp.int32, packed.shape, 1)
    return jnp.where(lane <= row, packed, 0.0)


def factor_of(packed, base):
    row = lax.broadcasted_iota(jnp.int32, packed.shape, 0) + base
    lane = lax.broadcasted_iota(jnp.int32, packed.shape, 1)
    return jnp.where(lane > row, packed, jnp.where(lane == row, 1.0 / packed, 0.0))


def peer(**place):
    return dict(device_id=place, device_id_type=pl.DeviceIdType.MESH)


def sweep_kernel(
    rows, columns, scale, choice, near, test, nugget,
    basis, missed, inner_basis, upper,
    panels, blocks, sample, moments, sums, inbox, work, pair,
    send_x, recv_x, send_y, recv_y, send_z, recv_z,
    send_c, recv_c, send_own, recv_own, send_near, recv_near, send_up, recv_up, here_sem,
):
    row, column = lax.axis_index("row"), lax.axis_index("col")
    leaves, size = near.shape[1], near.shape[2]
    piece = test.shape[0]
    width = moments.shape[1]
    levels = rows.bit_length() - 1
    corner = row % 4
    ends = jnp.logical_or(corner == 0, corner == 3)
    above = jnp.logical_and(ends, row + 4 < rows)
    below = jnp.logical_and(ends, row >= 4)
    z_out = jnp.where(corner == 0, row + 4, row - 4)
    has_out = jnp.where(corner == 0, above, below)
    has_in = jnp.where(corner == 0, below, above)

    barrier = pltpu.get_barrier_semaphore()
    for level in range(levels):
        pl.semaphore_signal(barrier, inc=1, **peer(row=row ^ (1 << level)))
    for shift in range(1, columns):
        pl.semaphore_signal(barrier, inc=1, **peer(col=(column + shift) % columns))

    @pl.when(above)
    def _():
        pl.semaphore_signal(barrier, inc=1, **peer(row=row + 4))

    @pl.when(below)
    def _():
        pl.semaphore_signal(barrier, inc=1, **peer(row=row - 4))

    extra = above.astype(jnp.int32) + below.astype(jnp.int32)
    pl.semaphore_wait(barrier, levels + columns - 1 + extra)

    cuts = CUTS
    part_rows = size // cuts
    chunks = piece * cuts

    def part(ref, *lead_and_chunk):
        *lead, chunk = lead_and_chunk
        at, cut = divmod(chunk, cuts)
        return ref.at[(*lead, at, pl.ds(cut * part_rows, part_rows))]

    def along(source, kind, chunk, send, recv, target):
        return pltpu.make_async_remote_copy(
            src_ref=source, dst_ref=part(panels, 0, kind, chunk),
            send_sem=send.at[chunk], recv_sem=recv.at[chunk], **peer(row=target),
        )

    def x_copy(chunk):
        return along(part(test, chunk), 1, chunk, send_x, recv_x, row ^ 1)

    def y_copy(chunk):
        return along(part(panels, 0, 1, chunk), 2, chunk, send_y, recv_y, row ^ 2)

    def z_copy(chunk):
        return along(part(panels, 0, 2, chunk), 3, chunk, send_z, recv_z, z_out)

    def c_copy(shift, kind, lane, chunk):
        return pltpu.make_async_remote_copy(
            src_ref=part(panels, 0, kind, chunk),
            dst_ref=part(panels, shift, kind, chunk),
            send_sem=send_c.at[shift - 1, lane, chunk],
            recv_sem=recv_c.at[shift - 1, lane, chunk],
            **peer(col=(column + shift) % columns),
        )

    def own_copy(shift):
        return pltpu.make_async_remote_copy(
            src_ref=test, dst_ref=panels.at[shift, 0],
            send_sem=send_own.at[shift - 1], recv_sem=recv_own.at[shift - 1],
            **peer(col=(column + shift) % columns),
        )

    def near_copy(shift):
        return pltpu.make_async_remote_copy(
            src_ref=near.at[0], dst_ref=blocks.at[shift],
            send_sem=send_near.at[shift - 1], recv_sem=recv_near.at[shift - 1],
            **peer(col=(column + shift) % columns),
        )

    shifts = range(1, columns)
    for chunk in range(chunks):
        x_copy(chunk).start()
    for shift in shifts:
        own_copy(shift).start()
        near_copy(shift).start()
    own_test = pltpu.make_async_copy(test, panels.at[0, 0], here_sem.at[0])
    own_near = pltpu.make_async_copy(near.at[0], blocks.at[0], here_sem.at[1])
    own_test.start()
    own_near.start()
    diagonal = lax.broadcasted_iota(jnp.int32, (size, size), 0) == lax.broadcasted_iota(
        jnp.int32, (size, size), 1
    )
    first = row * leaves

    def own_slot(leaf):
        slot = jnp.int32(0)
        for k in range(1, columns):
            slot = jnp.where(choice[k, leaf] == first + leaf, k, slot)
        return slot

    def own_product(leaf):
        variance = jnp.where(diagonal, nugget[pl.ds(leaf, 1), :], 0.0)
        holder = (column - leaf // piece + columns) % columns
        sample[leaf] = dot_three(
            blocks[own_slot(leaf), leaf] + variance, panels[holder, 0, leaf % piece], 1, 0
        )

    early = min(2, chunks + 1)
    share_leaves = -(-leaves // (chunks + 2 - early))
    for step in range(chunks + 2):
        if step == early:
            for shift in shifts:
                own_copy(shift).wait()
                near_copy(shift).wait()
            own_test.wait()
            own_near.wait()
        if step < chunks:
            x_copy(step).wait_recv()
            y_copy(step).start()
            for shift in shifts:
                c_copy(shift, 1, 0, step).start()
        if 1 <= step <= chunks:
            chunk = step - 1
            y_copy(chunk).wait_recv()

            @pl.when(has_out)
            def _():
                z_copy(chunk).start()

            @pl.when(jnp.logical_not(ends))
            def _():
                for shift in shifts:
                    c_copy(shift, 2, 1, chunk).start()

        if step >= 2:
            chunk = step - 2

            @pl.when(has_in)
            def _():
                z_copy(chunk).wait_recv()
                for shift in shifts:
                    c_copy(shift, 3, 1, chunk).start()

        if step >= early:
            start = (step - early) * share_leaves

            @pl.loop(start, min(start + share_leaves, leaves))
            def _(leaf):
                own_product(leaf)

    for chunk in range(chunks):
        x_copy(chunk).wait_send()
        y_copy(chunk).wait_send()
        for shift in shifts:
            c_copy(shift, 1, 0, chunk).wait()

        @pl.when(has_out)
        def _():
            z_copy(chunk).wait_send()

        @pl.when(jnp.logical_not(ends))
        def _():
            for shift in shifts:
                c_copy(shift, 2, 1, chunk).wait()

        @pl.when(has_in)
        def _():
            for shift in shifts:
                c_copy(shift, 3, 1, chunk).wait()

    corner_low = jnp.where(corner == 0, 3, jnp.where(corner == 2, 2, 1))
    corner_high = jnp.where(corner == 3, 3, jnp.where(corner == 1, 2, 1))
    grams_total = sums.at[0]
    grams_total[...] = jnp.zeros_like(grams_total)

    @pl.loop(0, leaves)
    def _(leaf):
        whole = sample[leaf]
        for other in range(1, columns):
            slot = lax.rem(own_slot(leaf) + other, columns)
            place = choice[slot, leaf] - first + leaves
            side, within = place // leaves, place % leaves
            kind = jnp.where(side == 0, corner_low, jnp.where(side == 1, 0, corner_high))
            holder = (column - within // piece + columns) % columns
            whole += dot_three(
                blocks[slot, leaf], panels[holder, kind, within % piece], 1, 0
            )
        sample[leaf] = whole
        both = dot(whole[:, :width], whole, 0, 0)
        moments[leaf] = both
        grams_total[...] += both

    share = 2 * width // columns
    side = column * share // width
    offset = pl.multiple_of(column * share % width, share)
    nodes = 2 * leaves - 1

    def climb(level):
        return pltpu.make_async_remote_copy(
            src_ref=sums.at[level], dst_ref=inbox.at[level],
            send_sem=send_up.at[level], recv_sem=recv_up.at[level],
            **peer(row=row ^ (1 << level)),
        )

    def arrive(level):
        stride = 1 << level
        climb(level).wait()
        both = sums[level] + inbox[level]
        sums[level + 1] = both
        if level + 1 < levels:
            climb(level + 1).start()

        @pl.when(row % (2 * stride) == stride)
        def _():
            load_augmented(pair, 0, both[:, :width])
            load_augmented(pair, 1, jnp.where(side == 0, inbox[level], sums[level])[:, :width])

    climb(0).start()
    for leaf in range(leaves):
        work[leaf] = moments[leaf, :, :width]
    for node in range(leaves, nodes):
        child = 2 * (node - leaves)
        work[node] = work[child] + work[child + 1]
    level = 0
    for top in range(0, width, STRIP):
        eliminate_packed(work, nodes, top)
        if level < levels:
            arrive(level)
            level += 1
    while level < levels:
        arrive(level)
        level += 1

    @pl.when(row == 0)
    def _():
        load_augmented(pair, 0, sums[levels, :, :width])
        load_augmented(pair, 1, sums[levels, :, :width])

    points = pl.ds(pl.multiple_of(column * share, share), share)

    def leaf_out(leaf):
        inverse = inverse_of(work[leaf])
        part_sample = sample[leaf, points, :]
        own = dot_three(inverse, part_sample[:, :width], 1, 1)
        basis[leaf] = own
        reduced = dot_three(inverse, moments[leaf, :, width:], 1, 0)
        missed[leaf] = part_sample[:, width:].T - dot_three(reduced, own, 0, 0)

    def node_out(node):
        child = 2 * (node - leaves) + side
        inner_basis[node - leaves] = dot_three(
            inverse_of(work[node]),
            factor_of(work[child, pl.ds(offset, share), :], offset), 1, 1,
        )

    jobs = [functools.partial(leaf_out, leaf) for leaf in range(leaves)]
    jobs += [functools.partial(node_out, node) for node in range(leaves, nodes)]
    strips = width // STRIP
    for at in range(strips):
        eliminate_strip(pair, 0, 2, at * STRIP)
        for job in jobs[at::strips]:
            job()
    inverse = pair[0, :, width:]
    total = sums[levels]
    if share % width:
        place_row = lax.broadcasted_iota(jnp.int32, (2 * width, share), 0)
        place_lane = lax.broadcasted_iota(jnp.int32, (2 * width, share), 1)
        chosen = jnp.where(place_row == place_lane + column * share, 1.0, 0.0)
        root = dot(total, chosen, 1, 0)
    else:
        root = jnp.where(side == 0, total[:, :width], total[:, width:])
    node = dot(inverse, pair[1, pl.ds(offset, share), :width], 1, 1)
    upper[0] = jnp.where(row == 0, dot(inverse, root, 1, 0) * scale, node)


def whole_spec():
    return pl.BlockSpec(memory_space=pltpu.VMEM)


def swept(choice, near, test, nugget, rows, columns, scale):
    leaves, size = near.shape[1], near.shape[2]
    piece, wide = test.shape[0], test.shape[2]
    width = wide // 2
    share = wide // columns
    nodes = 2 * leaves - 1
    levels = rows.bit_length() - 1
    chunks = piece * CUTS
    f32 = jnp.float32
    dma = pltpu.SemaphoreType.DMA
    smem = pl.BlockSpec(memory_space=pltpu.SMEM)
    anywhere = pl.BlockSpec(memory_space=pl.ANY)
    return pl.pallas_call(
        functools.partial(sweep_kernel, rows, columns, scale),
        in_specs=[smem, anywhere, anywhere, whole_spec()],
        out_specs=[whole_spec()] * 4,
        out_shape=[
            jax.ShapeDtypeStruct((count, width, share), f32)
            for count in (leaves, leaves, leaves - 1, 1)
        ],
        scratch_shapes=[
            pltpu.VMEM((columns, 4, piece, size, wide), f32),
            pltpu.VMEM((columns, leaves, size, size), f32),
            pltpu.VMEM((leaves, size, wide), f32),
            pltpu.VMEM((leaves, width, wide), f32),
            pltpu.VMEM((levels + 1, width, wide), f32),
            pltpu.VMEM((levels, width, wide), f32),
            pltpu.VMEM((nodes, width, width), f32),
            pltpu.VMEM((2, width, wide), f32),
        ]
        + [dma((chunks,))] * 6
        + [dma((columns - 1, 2, chunks))] * 2
        + [dma((columns - 1,))] * 4
        + [dma((levels,))] * 2
        + [dma((2,))],
        compiler_params=pltpu.CompilerParams(
            vmem_limit_bytes=LIMIT, collective_id=0, has_side_effects=True
        ),
    )(choice, near, test, nugget)


def around(block, axis):
    count = lax.axis_size(axis)
    parts = [block]
    for shift in range(1, count):
        route = [((i + shift) % count, i) for i in range(count)]
        parts.append(lax.ppermute(block, axis, route))
    return parts


def on_device(near_blocks, column_block, test_panels, nugget):
    leaves = near_blocks.shape[0]
    block = near_blocks.shape[2]
    rows = lax.axis_size("row")
    columns = lax.axis_size("col")
    choice = jnp.stack(around(column_block[:, 0], "col"))
    scale = 1.0 / math.sqrt(leaves * rows * block)
    outs = swept(
        choice, near_blocks.swapaxes(0, 1), test_panels, nugget, rows, columns, scale
    )
    return tuple(outs)


def solution(mesh):
    placed = (
        P("row", "col", None, None),
        P("row", "col"),
        P(("row", "col"), None, None),
        P("row", None),
    )
    return jax.shard_map(
        on_device,
        mesh=mesh,
        in_specs=placed,
        out_specs=(P("row", None, "col"),) * 4,
        check_vma=False,
    )
```

```python
import functools
import math

import jax
import jax.numpy as jnp
from jax import lax
from jax.experimental import pallas as pl
from jax.experimental.pallas import tpu as pltpu
from jax.sharding import PartitionSpec as P

STRIP = 32
SLAB = 8
CUTS = 2
GROUP = 4
LIMIT = 60 * 1024 * 1024


def dot(left, right, left_dim, right_dim):
    return lax.dot_general(
        left,
        right,
        (((left_dim,), (right_dim,)), ((), ())),
        precision=lax.Precision.HIGHEST,
        preferred_element_type=jnp.float32,
    )


def load_augmented(work, slot, gram):
    size = gram.shape[0]
    row = lax.broadcasted_iota(jnp.int32, (size, size), 0)
    lane = lax.broadcasted_iota(jnp.int32, (size, size), 1)
    work[slot, :, :size] = gram
    work[slot, :, size:] = jnp.where(row == lane, 1.0, 0.0)


def split(value):
    high = value.astype(jnp.bfloat16)
    return high, (value - high.astype(jnp.float32)).astype(jnp.bfloat16)


def dot_three(left, right, left_dim, right_dim):
    def one(a, b):
        return lax.dot_general(
            a, b, (((left_dim,), (right_dim,)), ((), ())), preferred_element_type=jnp.float32
        )

    left_high, left_low = split(left)
    right_high, right_low = split(right)
    return one(left_high, right_high) + (one(left_high, right_low) + one(left_low, right_high))


def eliminate_strip(work, first, count, top):
    size = work.shape[1]
    row = lax.broadcasted_iota(jnp.int32, (1, SLAB, size), 1)
    lane = lax.broadcasted_iota(jnp.int32, (1, SLAB, size), 2)
    own = pl.ds(first, count)
    shape = (count, SLAB, size)

    def spread(value):
        return jnp.broadcast_to(value, shape)

    slabs = [
        [
            work[own, top + at : top + at + SLAB, half : half + size]
            for half in (0, size)
        ]
        for at in range(0, STRIP, SLAB)
    ]
    for step in range(0, STRIP, GROUP):
        at, inner = divmod(step, SLAB)
        here = top + step
        columns = {
            later: [
                spread(slabs[later][0][:, :, here + k : here + k + 1]) for k in range(GROUP)
            ]
            for later in range(at, len(slabs))
        }
        pivots = [
            [
                spread(columns[at][k][:, inner + m : inner + m + 1, :]) if m >= k else None
                for m in range(GROUP)
            ]
            for k in range(GROUP)
        ]
        rows = [
            [spread(half[:, inner + k : inner + k + 1, :]) for half in slabs[at]]
            for k in range(GROUP)
        ]
        for k in range(GROUP):
            inverse = 1.0 / pivots[k][k]
            lower = {m: pivots[k][m] * inverse for m in range(k + 1, GROUP)}
            for t in range(k + 1, GROUP):
                for m in range(t, GROUP):
                    pivots[t][m] = pivots[t][m] - pivots[k][m] * lower[t]
                rows[t] = [x - lower[t] * y for x, y in zip(rows[t], rows[k])]
                for later in columns:
                    columns[later][t] = columns[later][t] - columns[later][k] * lower[t]
            scaled = [half * inverse for half in rows[k]]
            for later in columns:
                factor = columns[later][k]
                if later == at:
                    if inner + k == SLAB - 1:
                        continue
                    factor = jnp.where(row > inner + k, factor, 0.0)
                slabs[later] = [x - factor * y for x, y in zip(slabs[later], scaled)]
    for at, slab in enumerate(slabs):
        base = top + at * SLAB
        diagonal = jnp.sum(
            jnp.where(lane == row + base, slab[0], 0.0), axis=2, keepdims=True
        )
        scale = lax.rsqrt(diagonal)
        work[own, base : base + SLAB, :size] = jnp.where(lane >= row + base, slab[0] * scale, 0.0)
        work[own, base : base + SLAB, size:] = slab[1] * scale
    below = top + STRIP
    if below < size:
        for slot in range(first, first + count):
            strip = work[slot, top:below, :]
            work[slot, below:, :] -= dot(strip[:, below:size], strip, 0, 0)


def eliminate_packed(work, count, top):
    size = work.shape[1]
    below = top + STRIP
    row = lax.broadcasted_iota(jnp.int32, (1, SLAB, size), 1)
    lane = lax.broadcasted_iota(jnp.int32, (1, SLAB, size), 2)
    own = pl.ds(0, count)
    shape = (count, SLAB, size)
    slabs = [work[own, top + at : top + at + SLAB, :] for at in range(0, STRIP, SLAB)]
    pivots = [None] * len(slabs)
    for step in range(STRIP):
        at, inner = divmod(step, SLAB)
        here = top + step
        columns = [
            jnp.broadcast_to(slab[:, :, here : here + 1], shape) for slab in slabs[at:]
        ]
        pivot = jnp.broadcast_to(columns[0][:, inner : inner + 1, :], shape)
        inverse = 1.0 / pivot
        pivots[at] = pivot if inner == 0 else jnp.where(row >= inner, pivot, pivots[at])
        pivot_row = jnp.broadcast_to(slabs[at][:, inner : inner + 1, :], shape)
        scaled = jnp.where(lane == here, 1.0, pivot_row) * inverse
        for later in range(at, len(slabs)):
            factor, slab = columns[later - at], slabs[later]
            if later == at:
                factor = jnp.where(row > inner, factor, 0.0)
                keep = jnp.where(row > inner, 0.0, jnp.where(row == inner, 1.0, slab))
                slab = jnp.where(lane == here, keep, slab)
            else:
                slab = jnp.where(lane == here, 0.0, slab)
            slabs[later] = slab - factor * scaled
    for at, slab in enumerate(slabs):
        base = top + at * SLAB
        work[own, base : base + SLAB, :] = slab * lax.rsqrt(pivots[at])
    if below < size:
        strip_row = lax.broadcasted_iota(jnp.int32, (STRIP, size), 0) + top
        strip_lane = lax.broadcasted_iota(jnp.int32, (STRIP, size), 1)
        hide = jnp.logical_and(strip_lane < below, strip_lane > strip_row)
        rest_lane = lax.broadcasted_iota(jnp.int32, (size - below, size), 1)
        cleared = jnp.logical_and(rest_lane >= top, rest_lane < below)
        for slot in range(count):
            strip = work[slot, top:below, :]
            rest = jnp.where(cleared, 0.0, work[slot, below:, :])
            work[slot, below:, :] = rest - dot(
                strip[:, below:size], jnp.where(hide, 0.0, strip), 0, 0
            )


def inverse_of(packed):
    row = lax.broadcasted_iota(jnp.int32, packed.shape, 0)
    lane = lax.broadcasted_iota(jnp.int32, packed.shape, 1)
    return jnp.where(lane <= row, packed, 0.0)


def factor_of(packed, base):
    row = lax.broadcasted_iota(jnp.int32, packed.shape, 0) + base
    lane = lax.broadcasted_iota(jnp.int32, packed.shape, 1)
    return jnp.where(lane > row, packed, jnp.where(lane == row, 1.0 / packed, 0.0))


def peer(**place):
    return dict(device_id=place, device_id_type=pl.DeviceIdType.MESH)


def sweep_kernel(
    rows, columns, scale, choice, near, test, nugget,
    basis, missed, inner_basis, upper,
    panels, blocks, sample, moments, sums, inbox, work, pair,
    send_x, recv_x, send_y, recv_y, send_z, recv_z,
    send_c, recv_c, send_own, recv_own, send_near, recv_near, send_up, recv_up, send_side, recv_side, here_sem,
):
    row, column = lax.axis_index("row"), lax.axis_index("col")
    leaves, size = near.shape[1], near.shape[2]
    piece = test.shape[0]
    width = moments.shape[1]
    levels = rows.bit_length() - 1
    corner = row % 4
    ends = jnp.logical_or(corner == 0, corner == 3)
    above = jnp.logical_and(ends, row + 4 < rows)
    below = jnp.logical_and(ends, row >= 4)
    z_out = jnp.where(corner == 0, row + 4, row - 4)
    has_out = jnp.where(corner == 0, above, below)
    has_in = jnp.where(corner == 0, below, above)

    barrier = pltpu.get_barrier_semaphore()
    for level in range(levels):
        pl.semaphore_signal(barrier, inc=1, **peer(row=row ^ (1 << level)))
    for shift in range(1, columns):
        pl.semaphore_signal(barrier, inc=1, **peer(col=(column + shift) % columns))

    @pl.when(above)
    def _():
        pl.semaphore_signal(barrier, inc=1, **peer(row=row + 4))

    @pl.when(below)
    def _():
        pl.semaphore_signal(barrier, inc=1, **peer(row=row - 4))

    extra = above.astype(jnp.int32) + below.astype(jnp.int32)
    pl.semaphore_wait(barrier, levels + columns - 1 + extra)

    cuts = CUTS
    part_rows = size // cuts
    chunks = piece * cuts

    def part(ref, *lead_and_chunk):
        *lead, chunk = lead_and_chunk
        at, cut = divmod(chunk, cuts)
        return ref.at[(*lead, at, pl.ds(cut * part_rows, part_rows))]

    def along(source, kind, chunk, send, recv, target):
        return pltpu.make_async_remote_copy(
            src_ref=source, dst_ref=part(panels, 0, kind, chunk),
            send_sem=send.at[chunk], recv_sem=recv.at[chunk], **peer(row=target),
        )

    def x_copy(chunk):
        return along(part(test, chunk), 1, chunk, send_x, recv_x, row ^ 1)

    def y_copy(chunk):
        return along(part(panels, 0, 1, chunk), 2, chunk, send_y, recv_y, row ^ 2)

    def z_copy(chunk):
        return along(part(panels, 0, 2, chunk), 3, chunk, send_z, recv_z, z_out)

    def c_copy(shift, kind, lane, chunk):
        return pltpu.make_async_remote_copy(
            src_ref=part(panels, 0, kind, chunk),
            dst_ref=part(panels, shift, kind, chunk),
            send_sem=send_c.at[shift - 1, lane, chunk],
            recv_sem=recv_c.at[shift - 1, lane, chunk],
            **peer(col=(column + shift) % columns),
        )

    def own_copy(shift):
        return pltpu.make_async_remote_copy(
            src_ref=test, dst_ref=panels.at[shift, 0],
            send_sem=send_own.at[shift - 1], recv_sem=recv_own.at[shift - 1],
            **peer(col=(column + shift) % columns),
        )

    def near_copy(shift):
        return pltpu.make_async_remote_copy(
            src_ref=near.at[0], dst_ref=blocks.at[shift],
            send_sem=send_near.at[shift - 1], recv_sem=recv_near.at[shift - 1],
            **peer(col=(column + shift) % columns),
        )

    shifts = range(1, columns)
    for chunk in range(chunks):
        x_copy(chunk).start()
    for shift in shifts:
        own_copy(shift).start()
        near_copy(shift).start()
    own_test = pltpu.make_async_copy(test, panels.at[0, 0], here_sem.at[0])
    own_near = pltpu.make_async_copy(near.at[0], blocks.at[0], here_sem.at[1])
    own_test.start()
    own_near.start()
    diagonal = lax.broadcasted_iota(jnp.int32, (size, size), 0) == lax.broadcasted_iota(
        jnp.int32, (size, size), 1
    )
    first = row * leaves

    def own_slot(leaf):
        slot = jnp.int32(0)
        for k in range(1, columns):
            slot = jnp.where(choice[k, leaf] == first + leaf, k, slot)
        return slot

    def own_product(leaf):
        variance = jnp.where(diagonal, nugget[pl.ds(leaf, 1), :], 0.0)
        holder = (column - leaf // piece + columns) % columns
        sample[leaf] = dot_three(
            blocks[own_slot(leaf), leaf] + variance, panels[holder, 0, leaf % piece], 1, 0
        )

    early = min(2, chunks + 1)
    share_leaves = -(-leaves // (chunks + 2 - early))
    for step in range(chunks + 2):
        if step == early:
            for shift in shifts:
                own_copy(shift).wait()
                near_copy(shift).wait()
            own_test.wait()
            own_near.wait()
        if step < chunks:
            x_copy(step).wait_recv()
            y_copy(step).start()
            for shift in shifts:
                c_copy(shift, 1, 0, step).start()
        if 1 <= step <= chunks:
            chunk = step - 1
            y_copy(chunk).wait_recv()

            @pl.when(has_out)
            def _():
                z_copy(chunk).start()

            @pl.when(jnp.logical_not(ends))
            def _():
                for shift in shifts:
                    c_copy(shift, 2, 1, chunk).start()

        if step >= 2:
            chunk = step - 2

            @pl.when(has_in)
            def _():
                z_copy(chunk).wait_recv()
                for shift in shifts:
                    c_copy(shift, 3, 1, chunk).start()

        if step >= early:
            start = (step - early) * share_leaves

            @pl.loop(start, min(start + share_leaves, leaves))
            def _(leaf):
                own_product(leaf)

    for chunk in range(chunks):
        x_copy(chunk).wait_send()
        y_copy(chunk).wait_send()
        for shift in shifts:
            c_copy(shift, 1, 0, chunk).wait()

        @pl.when(has_out)
        def _():
            z_copy(chunk).wait_send()

        @pl.when(jnp.logical_not(ends))
        def _():
            for shift in shifts:
                c_copy(shift, 2, 1, chunk).wait()

        @pl.when(has_in)
        def _():
            for shift in shifts:
                c_copy(shift, 3, 1, chunk).wait()

    corner_low = jnp.where(corner == 0, 3, jnp.where(corner == 2, 2, 1))
    corner_high = jnp.where(corner == 3, 3, jnp.where(corner == 1, 2, 1))
    grams_total = sums.at[0]
    grams_total[...] = jnp.zeros_like(grams_total)

    @pl.loop(0, leaves)
    def _(leaf):
        whole = sample[leaf]
        for other in range(1, columns):
            slot = lax.rem(own_slot(leaf) + other, columns)
            place = choice[slot, leaf] - first + leaves
            side, within = place // leaves, place % leaves
            kind = jnp.where(side == 0, corner_low, jnp.where(side == 1, 0, corner_high))
            holder = (column - within // piece + columns) % columns
            whole += dot_three(
                blocks[slot, leaf], panels[holder, kind, within % piece], 1, 0
            )
        sample[leaf] = whole
        both = dot(whole[:, :width], whole, 0, 0)
        moments[leaf] = both
        grams_total[...] += both

    share = 2 * width // columns
    side = column * share // width
    offset = pl.multiple_of(column * share % width, share)
    nodes = 2 * leaves - 1

    band = width // columns

    def band_of(ref, level):
        return ref.at[level, pl.ds(pl.multiple_of(column * band, band), band)]

    def climb(level):
        return pltpu.make_async_remote_copy(
            src_ref=band_of(sums, level), dst_ref=band_of(inbox, level),
            send_sem=send_up.at[level], recv_sem=recv_up.at[level],
            **peer(row=row ^ (1 << level)),
        )

    def pass_on(level, shift):
        return pltpu.make_async_remote_copy(
            src_ref=band_of(inbox, level), dst_ref=band_of(inbox, level),
            send_sem=send_side.at[shift - 1, level], recv_sem=recv_side.at[shift - 1, level],
            **peer(col=(column + shift) % columns),
        )

    def arrive(level):
        climb(level).wait_recv()
        if level + 1 < levels:
            band_of(sums, level + 1)[...] = (
                band_of(sums, level)[...] + band_of(inbox, level)[...]
            )
            climb(level + 1).start()
        for shift in shifts:
            pass_on(level, shift).start()

    climb(0).start()
    for leaf in range(leaves):
        work[leaf] = moments[leaf, :, :width]
    for node in range(leaves, nodes):
        child = 2 * (node - leaves)
        work[node] = work[child] + work[child + 1]
    points = pl.ds(pl.multiple_of(column * share, share), share)

    def leaf_out(leaf):
        inverse = inverse_of(work[leaf])
        part_sample = sample[leaf, points, :]
        own = dot_three(inverse, part_sample[:, :width], 1, 1)
        basis[leaf] = own
        reduced = dot_three(inverse, moments[leaf, :, width:], 1, 0)
        missed[leaf] = part_sample[:, width:].T - dot_three(reduced, own, 0, 0)

    def node_out(node):
        child = 2 * (node - leaves) + side
        inner_basis[node - leaves] = dot_three(
            inverse_of(work[node]),
            factor_of(work[child, pl.ds(offset, share), :], offset), 1, 1,
        )

    jobs = [functools.partial(leaf_out, leaf) for leaf in range(leaves)]
    jobs += [functools.partial(node_out, node) for node in range(leaves, nodes)]
    half = len(jobs) // 2
    work_items = [
        [functools.partial(eliminate_packed, work, nodes, top)]
        for top in range(0, width, STRIP)
    ] + [jobs[:half], jobs[half:]]
    for level in range(levels):
        low, high = (len(work_items) * at // levels for at in (level, level + 1))
        for item in work_items[low:high]:
            for job in item:
                job()
        arrive(level)

    for level in range(levels):
        for shift in shifts:
            pass_on(level, shift).wait()
        climb(level).wait_send()
    for level in range(levels):
        stride = 1 << level
        both = sums[level] + inbox[level]
        sums[level + 1] = both

        @pl.when(row % (2 * stride) == stride)
        def _():
            load_augmented(pair, 0, both[:, :width])
            load_augmented(pair, 1, jnp.where(side == 0, inbox[level], sums[level])[:, :width])

    @pl.when(row == 0)
    def _():
        load_augmented(pair, 0, sums[levels, :, :width])
        load_augmented(pair, 1, sums[levels, :, :width])

    for top in range(0, width, STRIP):
        eliminate_strip(pair, 0, 2, top)
    inverse = pair[0, :, width:]
    total = sums[levels]
    if share % width:
        place_row = lax.broadcasted_iota(jnp.int32, (2 * width, share), 0)
        place_lane = lax.broadcasted_iota(jnp.int32, (2 * width, share), 1)
        chosen = jnp.where(place_row == place_lane + column * share, 1.0, 0.0)
        root = dot(total, chosen, 1, 0)
    else:
        root = jnp.where(side == 0, total[:, :width], total[:, width:])
    node = dot(inverse, pair[1, pl.ds(offset, share), :width], 1, 1)
    upper[0] = jnp.where(row == 0, dot(inverse, root, 1, 0) * scale, node)


def whole_spec():
    return pl.BlockSpec(memory_space=pltpu.VMEM)


def swept(choice, near, test, nugget, rows, columns, scale):
    leaves, size = near.shape[1], near.shape[2]
    piece, wide = test.shape[0], test.shape[2]
    width = wide // 2
    share = wide // columns
    nodes = 2 * leaves - 1
    levels = rows.bit_length() - 1
    chunks = piece * CUTS
    f32 = jnp.float32
    dma = pltpu.SemaphoreType.DMA
    smem = pl.BlockSpec(memory_space=pltpu.SMEM)
    anywhere = pl.BlockSpec(memory_space=pl.ANY)
    return pl.pallas_call(
        functools.partial(sweep_kernel, rows, columns, scale),
        in_specs=[smem, anywhere, anywhere, whole_spec()],
        out_specs=[whole_spec()] * 4,
        out_shape=[
            jax.ShapeDtypeStruct((count, width, share), f32)
            for count in (leaves, leaves, leaves - 1, 1)
        ],
        scratch_shapes=[
            pltpu.VMEM((columns, 4, piece, size, wide), f32),
            pltpu.VMEM((columns, leaves, size, size), f32),
            pltpu.VMEM((leaves, size, wide), f32),
            pltpu.VMEM((leaves, width, wide), f32),
            pltpu.VMEM((levels + 1, width, wide), f32),
            pltpu.VMEM((levels, width, wide), f32),
            pltpu.VMEM((nodes, width, width), f32),
            pltpu.VMEM((2, width, wide), f32),
        ]
        + [dma((chunks,))] * 6
        + [dma((columns - 1, 2, chunks))] * 2
        + [dma((columns - 1,))] * 4
        + [dma((levels,))] * 2
        + [dma((columns - 1, levels))] * 2
        + [dma((2,))],
        compiler_params=pltpu.CompilerParams(
            vmem_limit_bytes=LIMIT, collective_id=0, has_side_effects=True
        ),
    )(choice, near, test, nugget)


def around(block, axis):
    count = lax.axis_size(axis)
    parts = [block]
    for shift in range(1, count):
        route = [((i + shift) % count, i) for i in range(count)]
        parts.append(lax.ppermute(block, axis, route))
    return parts


def on_device(near_blocks, column_block, test_panels, nugget):
    leaves = near_blocks.shape[0]
    block = near_blocks.shape[2]
    rows = lax.axis_size("row")
    columns = lax.axis_size("col")
    choice = jnp.stack(around(column_block[:, 0], "col"))
    scale = 1.0 / math.sqrt(leaves * rows * block)
    outs = swept(
        choice, near_blocks.swapaxes(0, 1), test_panels, nugget, rows, columns, scale
    )
    return tuple(outs)


def solution(mesh):
    placed = (
        P("row", "col", None, None),
        P("row", "col"),
        P(("row", "col"), None, None),
        P("row", None),
    )
    return jax.shard_map(
        on_device,
        mesh=mesh,
        in_specs=placed,
        out_specs=(P("row", None, "col"),) * 4,
        check_vma=False,
    )
```
